256 devices in a mesh: sec: 64 (over z, x, core), mpo: 4 (over y).
Axes of the slice: x: 4, y: 4, z: 8, core: 2. Of those that a mesh axis runs over, the one named last changes fastest.
Arguments:
- wavefunction: bfloat16 [2048, 128, 128], P('sec'), may hold values from -100 to 100
- energy_shift: float32 [1], replicated, may hold values from 0.5 to 2
- left_env: bfloat16 [20, 2048, 128, 128], P('mpo', 'sec'), may hold values from -0.125 to 0.125
- right_env: bfloat16 [20, 2048, 128, 128], P('mpo', 'sec'), may hold values from -0.5 to 0.5
- target: int32 [20, 2048], P('mpo', 'sec'), may hold values from 0 to 2047, as said below
Outputs:
- second_image: bfloat16 [2048, 128, 128], P('sec')
The draws below stay inside these ranges and needn't reach their ends.
Inputs may be any that keep to these rules, and one draw needn't show every extreme that they name: `target`: for any device's blocks along sec and MPO terms of one device along mpo (terms j * 5 to (j + 1) * 5 - 1), at most 3 couplings point into the 32 blocks of one device, and that many do for some pair in every draw.
All inputs are finite; a program needn't handle non-finite values.
Results may differ from the reference program's by a relative error of at most 0.007.
Values may be sent and summed in bfloat16 or wider, within the bound.
A program may use at most 128 MiB of HBM per device.

```python
import jax
import jax.numpy as jnp
from jax import lax

B = 128
W = 20
BLK_DEV = 32
NBLK = 2048
N_SEC = 64
N_MPO = 4


def draw_wavefunction(key, part):
    key = jax.random.fold_in(key, 11)
    base_key = jax.random.fold_in(key, 0)
    position = jnp.arange(NBLK, dtype=jnp.float32) / max(NBLK - 1, 1)
    values = jnp.clip(jax.random.normal(base_key, (NBLK, B, B), jnp.float32), -5.0, 5.0)
    block_scale = jnp.exp(position * jnp.log(3.0))
    values = values * block_scale[:, None, None]
    return values.astype(jnp.bfloat16)


def draw_target(key, part):
    key = jax.random.fold_in(key, 23)
    terms_here = W // N_MPO
    perm_key, local_key = jax.random.split(key)
    perm_keys = jax.random.split(perm_key, N_MPO * N_SEC)
    orders = jax.vmap(lambda one_key: jax.random.permutation(one_key, N_SEC))(perm_keys)
    orders = orders.reshape(N_MPO, N_SEC, N_SEC).astype(jnp.int32)
    item_ids = (jnp.arange(terms_here * BLK_DEV, dtype=jnp.int32) % N_SEC).reshape(terms_here, BLK_DEV)
    owner_dev = orders[:, :, item_ids]
    local_pick = jax.random.randint(local_key, (N_MPO, N_SEC, terms_here, BLK_DEV), 0, BLK_DEV, jnp.int32)
    chosen = owner_dev * BLK_DEV + local_pick
    return jnp.transpose(chosen, (0, 2, 1, 3)).reshape(W, NBLK).astype(jnp.int32)


def levels(rng, shape, cuts, least, largest):
    factor_of = 1.0
    for axis_at, shards_of in cuts:
        steps = jax.random.uniform(jax.random.fold_in(jax.random.fold_in(rng, 6), axis_at), (shards_of,), jnp.float32, least / len(cuts), largest / len(cuts))
        factor_of = factor_of * jnp.repeat(jnp.exp(steps), shape[axis_at] // shards_of).reshape((-1,) + (1,) * (len(shape) - 1 - axis_at))
    return factor_of


def scatter_about(stream_key, extent, spread, limit, cuts=(), kind=jnp.bfloat16):
    entries = jax.random.normal(stream_key, extent, jnp.float32) * spread
    if len(cuts) > 0:
        entries = levels(stream_key, extent, cuts, -0.22, 0.18) * entries
    return jnp.clip(entries, min=-limit, max=limit).astype(kind)


def setup_inputs(seed: int = 0) -> dict:
    keys = jax.random.split(jax.random.key(seed), 6)
    wavefunction = draw_wavefunction(jax.random.fold_in(keys[5], 71), 0)
    energy_shift = jnp.clip(jax.random.uniform(keys[1], (1,), jnp.float32, 0.5, 2.0), 0.5, 2.0)
    left_env = scatter_about(keys[2], (W, NBLK, B, B), (W * B) ** -0.5, 0.125, ((0, 4), (1, 64)))
    right_env = scatter_about(keys[3], (W, NBLK, B, B), B ** -0.5, 0.5, ((0, 4), (1, 64)))
    target = draw_target(jax.random.fold_in(keys[5], 71), 0)
    return dict(wavefunction=wavefunction, energy_shift=energy_shift, left_env=left_env, right_env=right_env, target=target)


epsilon = 1e-06

def apply_hamiltonian(vector, left_env, right_env, target):
    vector_wide = vector.astype(jnp.float32)

    def add_term(accumulated, pieces):
        left_block, right_block, term_targets = pieces
        products = jnp.einsum('sij,sjk->sik', vector_wide, right_block.astype(jnp.float32)).astype(jnp.bfloat16)
        summed = jax.ops.segment_sum(products.astype(jnp.float32), term_targets.astype(jnp.int32), num_segments=NBLK)
        summed = summed.astype(jnp.bfloat16)
        contribution = jnp.einsum('tij,tjk->tik', left_block.astype(jnp.float32), summed.astype(jnp.float32))
        return (accumulated + contribution, None)
    start_zero = jnp.zeros((NBLK, B, B), jnp.float32)
    total, _ = lax.scan(add_term, start_zero, (left_env, right_env, target))
    return total

def reference(wavefunction, energy_shift, left_env, right_env, target):
    first_image = apply_hamiltonian(wavefunction, left_env, right_env, target)
    correction = first_image - energy_shift[0] * wavefunction.astype(jnp.float32)
    norm_corr = jnp.sqrt(jnp.mean(correction * correction) + epsilon)
    second_vector = (correction / norm_corr).astype(jnp.bfloat16)
    return apply_hamiltonian(second_vector, left_env, right_env, target).astype(jnp.bfloat16)
```

```python
import functools

import jax
import jax.numpy as jnp
from jax import lax
from jax.experimental import pallas as pl
from jax.experimental.pallas import tpu as pltpu
from jax.sharding import PartitionSpec as P

MESH = pl.DeviceIdType.MESH
EPSILON = 1e-06
NZ, NX, NC, NY = 8, 4, 2, 4
PEERS = NZ * NX * NC
CAP = 3
SLOTS = PEERS * CAP
B = 128
BLOCKS = 32
TERMS = 5
ITEMS = TERMS * BLOCKS
CHUNKS = 4
ROWS = B // CHUNKS
QUARTER = BLOCKS // NY
NT = (((1,), (1,)), ((), ()))
NN = (((1,), (0,)), ((), ()))


def coordinates():
    sec = lax.axis_index("sec")
    return sec // (NX * NC), (sec // NC) % NX, sec % NC, lax.axis_index("mpo")


def peer_of(offset, here):
    z, x, core, y = here
    dz, dx, dc = offset // (NX * NC), (offset // NC) % NX, offset % NC
    return (((z + dz) % NZ * NX + (x + dx) % NX) * NC + (core + dc) % NC, y)


def offset_at(i):
    zi, rest = i % NZ, (PEERS // NZ - 1) - i // NZ
    dist, sign = NZ // 2 - (zi + 1) // 2, 2 * (zi % 2) - 1
    return (dist * sign + NZ) % NZ * (NX * NC) + rest


def slot_tables(target, here):
    z, x, core, _ = here
    f32 = jnp.float32
    wide = jnp.concatenate([target, jnp.zeros((TERMS, B - BLOCKS), jnp.int32)], axis=1)
    padded = jnp.concatenate([wide, jnp.zeros((8 - TERMS, B), jnp.int32)], axis=0)
    device, local = padded >> 5, padded & (BLOCKS - 1)
    dz = ((device >> 3) - z + NZ) & (NZ - 1)
    dx = (((device >> 1) & (NX - 1)) - x + NX) & (NX - 1)
    dc = ((device & 1) - core + NC) & (NC - 1)
    term = lax.broadcasted_iota(jnp.int32, (8, B), 0)
    block = lax.broadcasted_iota(jnp.int32, (8, B), 1)
    real = block < BLOCKS
    offset = jnp.where(real, (dz * NX + dx) * NC + dc, PEERS).astype(f32)
    tag = (local * 8 + term).astype(f32)
    number = (block * 8 + term).astype(f32)
    fill = jnp.zeros((B - 8, B), f32)
    offset_t = jnp.concatenate([offset, fill], axis=0).T[:BLOCKS]
    number_t = jnp.concatenate([number, fill], axis=0).T[:BLOCKS]
    lanes = lax.broadcasted_iota(jnp.int32, (BLOCKS, 2 * B), 1).astype(f32)
    into = lax.broadcasted_iota(jnp.int32, (PEERS, B), 0).astype(f32)
    lane = lax.broadcasted_iota(jnp.int32, (PEERS, B), 1)
    source_col = lax.broadcasted_iota(jnp.int32, (BLOCKS, 1), 0).astype(f32)
    item = jnp.zeros((1, 2 * B), f32)
    source = jnp.zeros((1, 2 * B), f32)
    tags = jnp.full((PEERS, B), float(BLOCKS * 8), f32)
    for w in range(TERMS):
        rank_col = jnp.zeros((BLOCKS, 1), f32)
        rank_row = jnp.zeros((1, B), f32)
        for other in range(TERMS):
            met = (offset_t[:, w : w + 1] == offset[other : other + 1]) & (
                number[other : other + 1] < number_t[:, w : w + 1]
            )
            rank_col += jnp.sum(jnp.where(met, 1.0, 0.0), axis=1, keepdims=True)
            met = (offset_t[:, other : other + 1] == offset[w : w + 1]) & (
                number_t[:, other : other + 1] < number[w : w + 1]
            )
            rank_row += jnp.sum(jnp.where(met, 1.0, 0.0), axis=0, keepdims=True)
        slot = offset_t[:, w : w + 1] * CAP + rank_col
        at = jnp.where(lanes == slot, 1.0, 0.0)
        item += jnp.sum(at * (source_col + w * BLOCKS), axis=0, keepdims=True)
        source += jnp.sum(at * source_col, axis=0, keepdims=True)
        for k in range(CAP):
            met = (offset[w : w + 1] == into) & (rank_row == k)
            value = jnp.sum(jnp.where(met, tag[w : w + 1] + 1.0, 0.0), axis=1, keepdims=True)
            tags = jnp.where((lane == k) & (value > 0.0), value - 1.0, tags)
    return item.astype(jnp.int32), source.astype(jnp.int32), tags.astype(jnp.int32)


def main_kernel(
    energy, target_ref, v_ref, right_hbm, left_hbm, out_ref,
    tag_ref, slot_v, slot,
    right, left, right_t, going, arrived, segment, tags_in, table_v, table,
    rs_going, rs_arrived, own, v_t, second_t, out_t, ss_mine, ss_y, ss_x, ss_z,
    load_sem, tag_send, tag_recv, table_sem, go_send, go_recv, self_sem,
    rs_send, rs_recv, ag_send, ag_recv, ss_send, ss_recv,
):
    here = coordinates()
    z, x, core, y = here
    sec = (z * NX + x) * NC + core

    def y_peer(d):
        return (sec, (y + d) % NY)

    barrier = pltpu.get_barrier_semaphore()

    def greet(o, _):
        pl.semaphore_signal(barrier, inc=1, device_id=peer_of(o, here), device_id_type=MESH)
        return 0

    load_right = pltpu.make_async_copy(right_hbm, right, load_sem.at[0])
    load_left = pltpu.make_async_copy(left_hbm, left, load_sem.at[1])
    load_right.start()
    load_left.start()
    lax.fori_loop(1, PEERS, greet, 0)
    for d in range(1, NY):
        pl.semaphore_signal(barrier, inc=1, device_id=y_peer(d), device_id_type=MESH)
    item_row, source_row, tags = slot_tables(target_ref[...], here)
    slot_v[...] = jnp.concatenate([item_row, source_row, jnp.zeros((6, 2 * B), jnp.int32)], axis=0)
    to_scalar = pltpu.make_async_copy(slot_v, slot, table_sem)
    to_scalar.start()
    tag_ref[...] = jnp.broadcast_to(tags[:, None, :], (PEERS, 8, B))
    to_scalar.wait()
    load_right.wait()

    def remote(src, dst, send, recv, device):
        return pltpu.make_async_remote_copy(
            src_ref=src, dst_ref=dst, send_sem=send, recv_sem=recv, device_id=device, device_id_type=MESH
        )

    def products(o, m):
        for k in range(CAP):
            q = o * CAP + k
            if m == 0:
                block = right[jnp.clip(slot[0, q], 0, ITEMS - 1)].T
                right_t[q] = block
                product = lax.dot_general(block, v_ref[jnp.clip(slot[1, q], 0, BLOCKS - 1)], NT, preferred_element_type=jnp.float32)
            else:
                product = lax.dot_general(
                    right_t[q], second_t[jnp.clip(slot[1, q], 0, BLOCKS - 1)], NN, preferred_element_type=jnp.float32
                )
            product = product.astype(jnp.bfloat16)
            for c in range(CHUNKS):
                going[c, q] = product[c * ROWS : (c + 1) * ROWS]

    def send(o, m, c):
        slots = pl.ds(o * CAP, CAP)
        remote(
            going.at[c, slots], arrived[m * CHUNKS + c].at[slots],
            go_send.at[m, c], go_recv.at[m, c], peer_of(o, here),
        ).start()

    def send_tag(o):
        remote(tag_ref.at[o], tags_in.at[o], tag_send, tag_recv, peer_of(o, here)).start()

    def keep_own(m, c):
        pltpu.make_async_copy(
            going.at[c, pl.ds(0, CAP)], arrived[m * CHUNKS + c].at[pl.ds(0, CAP)], self_sem.at[m, c]
        ).start()

    def wait_own(m, c):
        pltpu.make_async_copy(
            going.at[c, pl.ds(0, CAP)], arrived[m * CHUNKS + c].at[pl.ds(0, CAP)], self_sem.at[m, c]
        ).wait()

    others = pl.ds(CAP, SLOTS - CAP)

    def wait_arrived(m, c):
        wait_own(m, c)
        into = arrived[m * CHUNKS + c].at[others]
        pltpu.make_async_copy(into, into, go_recv.at[m, c]).wait()

    def wait_sent(m, c):
        out_of = going.at[c, others]
        pltpu.make_async_copy(out_of, out_of, go_send.at[m, c]).wait()

    def send_all(m, c):
        def one(i, _):
            send(offset_at(i), m, c)
            return 0

        lax.fori_loop(0, PEERS - 1, one, 0)
        keep_own(m, c)

    early = 8

    def compute_first(i, _):
        products(offset_at(i), 0)
        return 0

    def send_first(i, _):
        send(offset_at(i), 0, 0)
        send_tag(offset_at(i))
        return 0

    def both_first(i, _):
        compute_first(i, 0)
        send_first(i, 0)
        return 0

    lax.fori_loop(0, early, compute_first, 0)
    pl.semaphore_wait(barrier, PEERS - 1 + NY - 1)
    lax.fori_loop(0, early, send_first, 0)
    lax.fori_loop(early, PEERS - 1, both_first, 0)
    products(0, 0)
    tags_in[0] = tag_ref[0]
    keep_own(0, 0)
    for c in range(1, CHUNKS):
        send_all(0, c)

    for j in range(QUARTER):
        v_t[j] = v_ref[y * QUARTER + j].astype(jnp.float32).T

    out_of = tag_ref.at[pl.ds(1, PEERS - 1)]
    into = tags_in.at[pl.ds(1, PEERS - 1)]
    pltpu.make_async_copy(into, into, tag_recv).wait()
    tag_all = jnp.max(tags_in[...], axis=1)
    order = lax.broadcasted_iota(jnp.int32, (PEERS, B), 0) * CAP + lax.broadcasted_iota(jnp.int32, (PEERS, B), 1)
    key = (tag_all * 256 + order).astype(jnp.float32)
    blank = jnp.full((B - PEERS, B), 1e9, jnp.float32)
    key_rows = jnp.concatenate([key, blank], axis=0).T
    tag_f = tag_all.astype(jnp.float32)
    block_f = (tag_all // 8).astype(jnp.float32)
    block_rows = jnp.concatenate([block_f, blank], axis=0).T
    lanes = lax.broadcasted_iota(jnp.int32, (PEERS, 2 * B), 1).astype(jnp.float32)
    order_f = order.astype(jnp.float32)
    perm = jnp.zeros((1, 2 * B), jnp.float32)
    tag_sorted = jnp.zeros((1, 2 * B), jnp.float32)
    follows = jnp.zeros((1, 2 * B), jnp.float32)
    last = jnp.zeros((1, 2 * B), jnp.float32)
    present = jnp.zeros((1, 2 * B), jnp.float32)
    for k in range(CAP):
        key_col = key[:, k : k + 1]
        block_col = block_f[:, k : k + 1]
        position = jnp.zeros((PEERS, 1), jnp.float32)
        before = jnp.zeros((PEERS, 1), jnp.float32)
        for other in range(CAP):
            less = key_rows[other : other + 1] < key_col
            same = block_rows[other : other + 1] == block_col
            position += jnp.sum(jnp.where(less, 1.0, 0.0), axis=1, keepdims=True)
            before += jnp.sum(jnp.where(less & same, 1.0, 0.0), axis=1, keepdims=True)
        here_p = jnp.where(lanes == position, 1.0, 0.0)
        perm += jnp.sum(here_p * order_f[:, k : k + 1], axis=0, keepdims=True)
        tag_sorted += jnp.sum(here_p * tag_f[:, k : k + 1], axis=0, keepdims=True)
        follows += jnp.sum(here_p * jnp.where(before > 0.0, 1.0, 0.0), axis=0, keepdims=True)
        last += jnp.sum(jnp.where(block_col <= lanes, 1.0, 0.0), axis=0, keepdims=True)
        present += jnp.sum(jnp.where(block_col == lanes, 1.0, 0.0), axis=0, keepdims=True)
    tag_i = tag_sorted.astype(jnp.int32)
    left_i = tag_i % 8 * BLOCKS + tag_i // 8
    rows = [
        perm.astype(jnp.int32),
        left_i,
        follows.astype(jnp.int32),
        jnp.maximum(last.astype(jnp.int32) - 1, 0),
        jnp.minimum(present.astype(jnp.int32), 1),
        jnp.zeros((3, 2 * B), jnp.int32),
    ]
    table_v[...] = jnp.concatenate(rows, axis=0)
    to_scalar = pltpu.make_async_copy(table_v, table, table_sem)
    to_scalar.start()
    to_scalar.wait()
    load_left.wait()

    def left_products(m, c):
        blocks = arrived[m * CHUNKS + c]

        def step(p, total):
            product = lax.dot_general(
                blocks[jnp.clip(table[0, p], 0, SLOTS - 1)], left[jnp.clip(table[1, p], 0, ITEMS - 1)], NT, preferred_element_type=jnp.float32
            )
            total = jnp.where(table[2, p] > 0, total, 0.0) + product
            segment[p] = total
            return total

        lax.fori_loop(0, SLOTS, step, jnp.zeros((ROWS, B), jnp.float32), unroll=8)

        def finish(t, _):
            value = jnp.where(table[4, t] > 0, segment[jnp.clip(table[3, t], 0, SLOTS - 1)], 0.0)
            rs_going[m * CHUNKS + c, t] = value.astype(jnp.bfloat16)
            return 0

        lax.fori_loop(0, BLOCKS, finish, 0, unroll=4)

        def finish_own(j, _):
            t = y * QUARTER + j
            own[c, j] = jnp.where(table[4, t] > 0, segment[jnp.clip(table[3, t], 0, SLOTS - 1)], 0.0)
            return 0

        lax.fori_loop(0, QUARTER, finish_own, 0, unroll=4)

    def scatter_y(m, c, d):
        quarter = (y + d) % NY * QUARTER
        return remote(
            rs_going.at[m * CHUNKS + c, pl.ds(quarter, QUARTER)], rs_arrived.at[m * CHUNKS + c, d - 1],
            rs_send.at[m * CHUNKS + c, d - 1], rs_recv.at[m * CHUNKS + c, d - 1], y_peer(d),
        )

    def sum_y(m, c):
        total = own[c]
        for d in range(1, NY):
            scatter_y(m, c, d).wait_recv()
            total += rs_arrived[m * CHUNKS + c, d - 1].astype(jnp.float32)
        return total

    def gather_y(m, c, d):
        where = (second_t, out_t)[m].at[pl.ds(y * QUARTER, QUARTER), pl.ds(c * ROWS, ROWS)]
        return remote(where, where, ag_send.at[m * CHUNKS + c, d - 1], ag_recv.at[m * CHUNKS + c, d - 1], y_peer(d))

    def arrives_y(m, c, d):
        quarter = (y - d + NY) % NY * QUARTER
        where = (second_t, out_t)[m].at[pl.ds(quarter, QUARTER), pl.ds(c * ROWS, ROWS)]
        return remote(where, where, ag_send.at[m * CHUNKS + c, d - 1], ag_recv.at[m * CHUNKS + c, d - 1], y_peer(d))

    shift = energy[0]
    ss_mine[0] = jnp.zeros((8, B), jnp.float32)

    def correct(c):
        value = sum_y(0, c) - shift * v_t[:, c * ROWS : (c + 1) * ROWS, :]
        ss_mine[0] += jnp.sum((value * value).reshape(QUARTER * ROWS // 8, 8, B), axis=0)
        second_t[pl.ds(y * QUARTER, QUARTER), pl.ds(c * ROWS, ROWS)] = value.astype(jnp.bfloat16)
        for d in range(1, NY):
            gather_y(0, c, d).start()

    for c in range(CHUNKS):
        wait_arrived(0, c)
        left_products(0, c)
        for d in range(1, NY):
            scatter_y(0, c, d).start()
        if c > 0:
            correct(c - 1)
    correct(CHUNKS - 1)
    for c in range(CHUNKS):
        wait_sent(0, c)
        for d in range(1, NY):
            arrives_y(0, c, d).wait_recv()

    def both_second(i, _):
        products(offset_at(i), 1)
        send(offset_at(i), 1, 0)
        return 0

    lax.fori_loop(0, PEERS - 1, both_second, 0)
    products(0, 1)
    keep_own(1, 0)
    for c in range(1, CHUNKS):
        send_all(1, c)

    def exchange(stage, buffer, count, device):
        copies = [
            remote(ss_mine.at[stage], buffer.at[d - 1], ss_send.at[stage, d - 1], ss_recv.at[stage, d - 1], device(d))
            for d in range(1, count)
        ]
        for copy in copies:
            copy.start()
        total = ss_mine[stage]
        for d, copy in enumerate(copies):
            copy.wait()
            total += buffer[d]
        return total

    ss_mine[1] = exchange(0, ss_y, NY, y_peer)
    ss_mine[2] = exchange(1, ss_x, NX * NC, lambda d: peer_of(jnp.int32(d), here))
    squares = exchange(2, ss_z, NZ, lambda d: peer_of(jnp.int32(d * NX * NC), here))
    cells = PEERS * BLOCKS * B * B
    inverse = 1.0 / jnp.sqrt(jnp.sum(squares, keepdims=True) / cells + EPSILON)

    def result(c):
        value = sum_y(1, c) * inverse
        out_t[pl.ds(y * QUARTER, QUARTER), pl.ds(c * ROWS, ROWS)] = value.astype(jnp.bfloat16)
        for d in range(1, NY):
            gather_y(1, c, d).start()

    for c in range(CHUNKS):
        wait_arrived(1, c)
        left_products(1, c)
        for d in range(1, NY):
            scatter_y(1, c, d).start()
        if c > 0:
            result(c - 1)
    result(CHUNKS - 1)
    for c in range(CHUNKS):
        for d in range(1, NY):
            arrives_y(1, c, d).wait_recv()

    def turn(t, _):
        out_ref[t] = out_t[t].T
        return 0

    lax.fori_loop(0, BLOCKS, turn, 0, unroll=4)
    pltpu.make_async_copy(out_of, out_of, tag_send).wait()
    for c in range(CHUNKS):
        wait_sent(1, c)
        for m in range(2):
            for d in range(1, NY):
                scatter_y(m, c, d).wait_send()
                gather_y(m, c, d).wait_send()


def body(wavefunction, energy_shift, left_env, right_env, target):
    smem, vmem = pl.BlockSpec(memory_space=pltpu.SMEM), pl.BlockSpec(memory_space=pltpu.VMEM)
    hbm = pl.BlockSpec(memory_space=pl.ANY)
    bf16, f32 = jnp.bfloat16, jnp.float32
    dma, all_chunks = pltpu.SemaphoreType.DMA, 2 * CHUNKS
    scratch = [
        pltpu.VMEM((PEERS, 8, B), jnp.int32),
        pltpu.VMEM((8, 2 * B), jnp.int32),
        pltpu.SMEM((8, 2 * B), jnp.int32),
        pltpu.VMEM((ITEMS, B, B), bf16),
        pltpu.VMEM((ITEMS, B, B), bf16),
        pltpu.VMEM((SLOTS, B, B), bf16),
        pltpu.VMEM((CHUNKS, SLOTS, ROWS, B), bf16),
        [pltpu.VMEM((SLOTS, ROWS, B), bf16) for _ in range(all_chunks)],
        pltpu.VMEM((SLOTS, ROWS, B), f32),
        pltpu.VMEM((PEERS, 8, B), jnp.int32),
        pltpu.VMEM((8, 2 * B), jnp.int32),
        pltpu.SMEM((8, 2 * B), jnp.int32),
        pltpu.VMEM((all_chunks, BLOCKS, ROWS, B), bf16),
        pltpu.VMEM((all_chunks, NY - 1, QUARTER, ROWS, B), bf16),
        pltpu.VMEM((CHUNKS, QUARTER, ROWS, B), f32),
        pltpu.VMEM((QUARTER, B, B), f32),
        pltpu.VMEM((BLOCKS, B, B), bf16),
        pltpu.VMEM((BLOCKS, B, B), bf16),
        pltpu.VMEM((3, 8, B), f32),
        pltpu.VMEM((NY - 1, 8, B), f32),
        pltpu.VMEM((NX * NC - 1, 8, B), f32),
        pltpu.VMEM((NZ - 1, 8, B), f32),
        dma((2,)),
        dma,
        dma,
        dma,
        dma((2, CHUNKS)),
        dma((2, CHUNKS)),
        dma((2, CHUNKS)),
        dma((all_chunks, NY - 1)),
        dma((all_chunks, NY - 1)),
        dma((all_chunks, NY - 1)),
        dma((all_chunks, NY - 1)),
        dma((3, NZ - 1)),
        dma((3, NZ - 1)),
    ]
    return pl.pallas_call(
        main_kernel,
        out_shape=jax.ShapeDtypeStruct((BLOCKS, B, B), bf16),
        in_specs=[smem, vmem, vmem, hbm, hbm],
        out_specs=vmem,
        scratch_shapes=scratch,
        compiler_params=pltpu.CompilerParams(
            collective_id=0, has_side_effects=True, vmem_limit_bytes=58 * 2**20
        ),
        name="davidson",
    )(
        energy_shift, target, wavefunction,
        right_env.reshape(ITEMS, B, B), left_env.reshape(ITEMS, B, B),
    )


def solution(mesh):
    placed = (
        P("sec", None, None),
        P(),
        P("mpo", "sec", None, None),
        P("mpo", "sec", None, None),
        P("mpo", "sec"),
    )
    return jax.shard_map(
        body, mesh=mesh, in_specs=placed, out_specs=P("sec", None, None), check_vma=False
    )
```

```python
import functools

import jax
import jax.numpy as jnp
from jax import lax
from jax.experimental import pallas as pl
from jax.experimental.pallas import tpu as pltpu
from jax.sharding import PartitionSpec as P

MESH = pl.DeviceIdType.MESH
EPSILON = 1e-06
NZ, NX, NC, NY = 8, 4, 2, 4
PEERS = NZ * NX * NC
CAP = 3
SLOTS = PEERS * CAP
B = 128
BLOCKS = 32
TERMS = 5
ITEMS = TERMS * BLOCKS
ROWS = (48, 48, 16, 16)
START = tuple(sum(ROWS[:c]) for c in range(len(ROWS)))
CHUNKS = len(ROWS)
QUARTER = BLOCKS // NY
NT = (((1,), (1,)), ((), ()))
NN = (((1,), (0,)), ((), ()))


def coordinates():
    sec = lax.axis_index("sec")
    return sec // (NX * NC), (sec // NC) % NX, sec % NC, lax.axis_index("mpo")


def peer_of(offset, here):
    z, x, core, y = here
    dz, dx, dc = offset // (NX * NC), (offset // NC) % NX, offset % NC
    return (((z + dz) % NZ * NX + (x + dx) % NX) * NC + (core + dc) % NC, y)


def offset_at(i):
    zi, rest = i % NZ, (PEERS // NZ - 1) - i // NZ
    dist, sign = NZ // 2 - (zi + 1) // 2, 2 * (zi % 2) - 1
    return (dist * sign + NZ) % NZ * (NX * NC) + rest


def slot_tables(target, here):
    z, x, core, _ = here
    f32 = jnp.float32
    wide = jnp.concatenate([target, jnp.zeros((TERMS, B - BLOCKS), jnp.int32)], axis=1)
    padded = jnp.concatenate([wide, jnp.zeros((8 - TERMS, B), jnp.int32)], axis=0)
    device, local = padded >> 5, padded & (BLOCKS - 1)
    dz = ((device >> 3) - z + NZ) & (NZ - 1)
    dx = (((device >> 1) & (NX - 1)) - x + NX) & (NX - 1)
    dc = ((device & 1) - core + NC) & (NC - 1)
    term = lax.broadcasted_iota(jnp.int32, (8, B), 0)
    block = lax.broadcasted_iota(jnp.int32, (8, B), 1)
    real = block < BLOCKS
    offset = jnp.where(real, (dz * NX + dx) * NC + dc, PEERS).astype(f32)
    tag = (local * 8 + term).astype(f32)
    number = (block * 8 + term).astype(f32)
    fill = jnp.zeros((B - 8, B), f32)
    offset_t = jnp.concatenate([offset, fill], axis=0).T[:BLOCKS]
    number_t = jnp.concatenate([number, fill], axis=0).T[:BLOCKS]
    lanes = lax.broadcasted_iota(jnp.int32, (BLOCKS, 2 * B), 1).astype(f32)
    into = lax.broadcasted_iota(jnp.int32, (PEERS, B), 0).astype(f32)
    lane = lax.broadcasted_iota(jnp.int32, (PEERS, B), 1)
    source_col = lax.broadcasted_iota(jnp.int32, (BLOCKS, 1), 0).astype(f32)
    item = jnp.zeros((1, 2 * B), f32)
    source = jnp.zeros((1, 2 * B), f32)
    tags = jnp.full((PEERS, B), float(BLOCKS * 8), f32)
    for w in range(TERMS):
        rank_col = jnp.zeros((BLOCKS, 1), f32)
        rank_row = jnp.zeros((1, B), f32)
        for other in range(TERMS):
            met = (offset_t[:, w : w + 1] == offset[other : other + 1]) & (
                number[other : other + 1] < number_t[:, w : w + 1]
            )
            rank_col += jnp.sum(jnp.where(met, 1.0, 0.0), axis=1, keepdims=True)
            met = (offset_t[:, other : other + 1] == offset[w : w + 1]) & (
                number_t[:, other : other + 1] < number[w : w + 1]
            )
            rank_row += jnp.sum(jnp.where(met, 1.0, 0.0), axis=0, keepdims=True)
        slot = offset_t[:, w : w + 1] * CAP + rank_col
        at = jnp.where(lanes == slot, 1.0, 0.0)
        item += jnp.sum(at * (source_col + w * BLOCKS), axis=0, keepdims=True)
        source += jnp.sum(at * source_col, axis=0, keepdims=True)
        for k in range(CAP):
            met = (offset[w : w + 1] == into) & (rank_row == k)
            value = jnp.sum(jnp.where(met, tag[w : w + 1] + 1.0, 0.0), axis=1, keepdims=True)
            tags = jnp.where((lane == k) & (value > 0.0), value - 1.0, tags)
    return item.astype(jnp.int32), source.astype(jnp.int32), tags.astype(jnp.int32)


def main_kernel(
    energy, target_ref, v_ref, right_hbm, left_hbm, out_ref,
    tag_ref, slot_v, slot,
    right, left, right_t, going, arrived, segment, tags_in, table_v, table,
    rs_going, rs_arrived, own, v_t, second_t, ss_mine, ss_y, ss_x, ss_z,
    load_sem, tag_send, tag_recv, table_sem, go_send, go_recv, self_sem,
    rs_send, rs_recv, ag_send, ag_recv, ss_send, ss_recv,
):
    here = coordinates()
    z, x, core, y = here
    sec = (z * NX + x) * NC + core

    def y_peer(d):
        return (sec, (y + d) % NY)

    barrier = pltpu.get_barrier_semaphore()

    def greet(o, _):
        pl.semaphore_signal(barrier, inc=1, device_id=peer_of(o, here), device_id_type=MESH)
        return 0

    load_right = pltpu.make_async_copy(right_hbm, right, load_sem.at[0])
    load_left = pltpu.make_async_copy(left_hbm, left, load_sem.at[1])
    load_right.start()
    load_left.start()
    lax.fori_loop(1, PEERS, greet, 0)
    for d in range(1, NY):
        pl.semaphore_signal(barrier, inc=1, device_id=y_peer(d), device_id_type=MESH)
    item_row, source_row, tags = slot_tables(target_ref[...], here)
    slot_v[...] = jnp.concatenate([item_row, source_row, jnp.zeros((6, 2 * B), jnp.int32)], axis=0)
    to_scalar = pltpu.make_async_copy(slot_v, slot, table_sem)
    to_scalar.start()
    tag_ref[...] = jnp.broadcast_to(tags[:, None, :], (PEERS, 8, B))
    to_scalar.wait()
    load_right.wait()

    def remote(src, dst, send, recv, device):
        return pltpu.make_async_remote_copy(
            src_ref=src, dst_ref=dst, send_sem=send, recv_sem=recv, device_id=device, device_id_type=MESH
        )

    def products(o, m):
        for k in range(CAP):
            q = o * CAP + k
            if m == 0:
                block = right[jnp.clip(slot[0, q], 0, ITEMS - 1)].T
                right_t[q] = block
                product = lax.dot_general(block, v_ref[jnp.clip(slot[1, q], 0, BLOCKS - 1)], NT, preferred_element_type=jnp.float32)
            else:
                product = lax.dot_general(
                    right_t[q], second_t[jnp.clip(slot[1, q], 0, BLOCKS - 1)], NN, preferred_element_type=jnp.float32
                )
            product = product.astype(jnp.bfloat16)
            for c in range(CHUNKS):
                going[c][q] = product[START[c] : START[c] + ROWS[c]]

    def send(o, m, c):
        slots = pl.ds(o * CAP, CAP)
        remote(
            going[c].at[slots], arrived[m * CHUNKS + c].at[slots],
            go_send.at[m, c], go_recv.at[m, c], peer_of(o, here),
        ).start()

    def send_tag(o):
        remote(tag_ref.at[o], tags_in.at[o], tag_send, tag_recv, peer_of(o, here)).start()

    def keep_own(m, c):
        pltpu.make_async_copy(
            going[c].at[pl.ds(0, CAP)], arrived[m * CHUNKS + c].at[pl.ds(0, CAP)], self_sem.at[m, c]
        ).start()

    def wait_own(m, c):
        pltpu.make_async_copy(
            going[c].at[pl.ds(0, CAP)], arrived[m * CHUNKS + c].at[pl.ds(0, CAP)], self_sem.at[m, c]
        ).wait()

    others = pl.ds(CAP, SLOTS - CAP)

    def wait_arrived(m, c):
        wait_own(m, c)
        into = arrived[m * CHUNKS + c].at[others]
        pltpu.make_async_copy(into, into, go_recv.at[m, c]).wait()

    def wait_sent(m, c):
        out_of = going[c].at[others]
        pltpu.make_async_copy(out_of, out_of, go_send.at[m, c]).wait()

    def send_all(m, c):
        def one(i, _):
            send(offset_at(i), m, c)
            return 0

        lax.fori_loop(0, PEERS - 1, one, 0)
        keep_own(m, c)

    early = 16

    def compute_first(i, _):
        products(offset_at(i), 0)
        return 0

    def send_first(i, _):
        send(offset_at(i), 0, 0)
        send_tag(offset_at(i))
        return 0

    def both_first(i, _):
        compute_first(i, 0)
        send_first(i, 0)
        return 0

    lax.fori_loop(0, early, compute_first, 0)
    pl.semaphore_wait(barrier, PEERS - 1 + NY - 1)
    lax.fori_loop(0, early, send_first, 0)
    lax.fori_loop(early, PEERS - 1, both_first, 0)
    products(0, 0)
    tags_in[0] = tag_ref[0]
    keep_own(0, 0)
    send_all(0, 1)

    for j in range(QUARTER):
        v_t[j] = v_ref[y * QUARTER + j].astype(jnp.float32).T

    out_of = tag_ref.at[pl.ds(1, PEERS - 1)]
    into = tags_in.at[pl.ds(1, PEERS - 1)]
    pltpu.make_async_copy(into, into, tag_recv).wait()
    tag_all = jnp.max(tags_in[...], axis=1)
    order = lax.broadcasted_iota(jnp.int32, (PEERS, B), 0) * CAP + lax.broadcasted_iota(jnp.int32, (PEERS, B), 1)
    key = (tag_all * 256 + order).astype(jnp.float32)
    blank = jnp.full((B - PEERS, B), 1e9, jnp.float32)
    key_rows = jnp.concatenate([key, blank], axis=0).T
    tag_f = tag_all.astype(jnp.float32)
    block_f = (tag_all // 8).astype(jnp.float32)
    block_rows = jnp.concatenate([block_f, blank], axis=0).T
    lanes = lax.broadcasted_iota(jnp.int32, (PEERS, 2 * B), 1).astype(jnp.float32)
    order_f = order.astype(jnp.float32)
    perm = jnp.zeros((1, 2 * B), jnp.float32)
    tag_sorted = jnp.zeros((1, 2 * B), jnp.float32)
    follows = jnp.zeros((1, 2 * B), jnp.float32)
    last = jnp.zeros((1, 2 * B), jnp.float32)
    present = jnp.zeros((1, 2 * B), jnp.float32)
    for k in range(CAP):
        key_col = key[:, k : k + 1]
        block_col = block_f[:, k : k + 1]
        position = jnp.zeros((PEERS, 1), jnp.float32)
        before = jnp.zeros((PEERS, 1), jnp.float32)
        for other in range(CAP):
            less = key_rows[other : other + 1] < key_col
            same = block_rows[other : other + 1] == block_col
            position += jnp.sum(jnp.where(less, 1.0, 0.0), axis=1, keepdims=True)
            before += jnp.sum(jnp.where(less & same, 1.0, 0.0), axis=1, keepdims=True)
        here_p = jnp.where(lanes == position, 1.0, 0.0)
        perm += jnp.sum(here_p * order_f[:, k : k + 1], axis=0, keepdims=True)
        tag_sorted += jnp.sum(here_p * tag_f[:, k : k + 1], axis=0, keepdims=True)
        follows += jnp.sum(here_p * jnp.where(before > 0.0, 1.0, 0.0), axis=0, keepdims=True)
        last += jnp.sum(jnp.where(block_col <= lanes, 1.0, 0.0), axis=0, keepdims=True)
        present += jnp.sum(jnp.where(block_col == lanes, 1.0, 0.0), axis=0, keepdims=True)
    tag_i = tag_sorted.astype(jnp.int32)
    left_i = tag_i % 8 * BLOCKS + tag_i // 8
    rows = [
        perm.astype(jnp.int32),
        left_i,
        follows.astype(jnp.int32),
        jnp.maximum(last.astype(jnp.int32) - 1, 0),
        jnp.minimum(present.astype(jnp.int32), 1),
        jnp.zeros((3, 2 * B), jnp.int32),
    ]
    table_v[...] = jnp.concatenate(rows, axis=0)
    to_scalar = pltpu.make_async_copy(table_v, table, table_sem)
    to_scalar.start()
    to_scalar.wait()
    load_left.wait()

    def turn_left(n, _):
        left[n] = left[n].T
        return 0

    lax.fori_loop(0, ITEMS, turn_left, 0, unroll=4)

    def left_products(m, c):
        blocks = arrived[m * CHUNKS + c]

        def step(p, total):
            product = lax.dot_general(
                blocks[jnp.clip(table[0, p], 0, SLOTS - 1)], left[jnp.clip(table[1, p], 0, ITEMS - 1)], NN, preferred_element_type=jnp.float32
            )
            total = jnp.where(table[2, p] > 0, total, 0.0) + product
            segment[p, : ROWS[c]] = total
            return total

        lax.fori_loop(0, SLOTS, step, jnp.zeros((ROWS[c], B), jnp.float32), unroll=8)

        def finish(t, _):
            value = jnp.where(table[4, t] > 0, segment[jnp.clip(table[3, t], 0, SLOTS - 1), : ROWS[c]], 0.0)
            rs_going[m * CHUNKS + c][t] = value.astype(jnp.bfloat16)
            return 0

        lax.fori_loop(0, BLOCKS, finish, 0, unroll=4)

    def own_quarter(c):
        def finish_own(j, _):
            t = y * QUARTER + j
            own[c][j] = jnp.where(table[4, t] > 0, segment[jnp.clip(table[3, t], 0, SLOTS - 1), : ROWS[c]], 0.0)
            return 0

        lax.fori_loop(0, QUARTER, finish_own, 0, unroll=4)

    def scatter_y(m, c, d):
        quarter = (y + d) % NY * QUARTER
        return remote(
            rs_going[m * CHUNKS + c].at[pl.ds(quarter, QUARTER)], rs_arrived[m * CHUNKS + c].at[d - 1],
            rs_send.at[m * CHUNKS + c, d - 1], rs_recv.at[m * CHUNKS + c, d - 1], y_peer(d),
        )

    def sum_y(m, c):
        total = own[c][...]
        for d in range(1, NY):
            scatter_y(m, c, d).wait_recv()
            total += rs_arrived[m * CHUNKS + c][d - 1].astype(jnp.float32)
        return total

    def gather_y(m, c, d):
        where = (second_t, out_ref)[m].at[pl.ds(y * QUARTER, QUARTER), pl.ds(START[c], ROWS[c])]
        return remote(where, where, ag_send.at[m * CHUNKS + c, d - 1], ag_recv.at[m * CHUNKS + c, d - 1], y_peer(d))

    def arrives_y(m, c, d):
        quarter = (y - d + NY) % NY * QUARTER
        where = (second_t, out_ref)[m].at[pl.ds(quarter, QUARTER), pl.ds(START[c], ROWS[c])]
        return remote(where, where, ag_send.at[m * CHUNKS + c, d - 1], ag_recv.at[m * CHUNKS + c, d - 1], y_peer(d))

    shift = energy[0]
    ss_mine[0] = jnp.zeros((8, B), jnp.float32)

    def correct(c):
        value = sum_y(0, c) - shift * v_t[:, START[c] : START[c] + ROWS[c], :]
        ss_mine[0] += jnp.sum((value * value).reshape(QUARTER * ROWS[c] // 8, 8, B), axis=0)
        second_t[pl.ds(y * QUARTER, QUARTER), pl.ds(START[c], ROWS[c])] = value.astype(jnp.bfloat16)
        for d in range(1, NY):
            gather_y(0, c, d).start()

    def exchange(stage):
        buffer, count, device = (
            (ss_y, NY, y_peer),
            (ss_x, NX * NC, lambda d: peer_of(jnp.int32(d), here)),
            (ss_z, NZ, lambda d: peer_of(jnp.int32(d * NX * NC), here)),
        )[stage]
        return buffer, [
            remote(ss_mine.at[stage], buffer.at[d - 1], ss_send.at[stage, d - 1], ss_recv.at[stage, d - 1], device(d))
            for d in range(1, count)
        ]

    def start_exchange(stage):
        for copy in exchange(stage)[1]:
            copy.start()

    def finish_exchange(stage):
        buffer, copies = exchange(stage)
        total = ss_mine[stage]
        for d, copy in enumerate(copies):
            copy.wait()
            total += buffer[d]
        return total

    for c in range(CHUNKS):
        wait_arrived(0, c)
        left_products(0, c)
        for d in range(1, NY):
            scatter_y(0, c, d).start()
        own_quarter(c)
        if c + 2 < CHUNKS:
            send_all(0, c + 2)
        if c > 0:
            correct(c - 1)
    correct(CHUNKS - 1)
    start_exchange(0)
    for c in range(CHUNKS):
        wait_sent(0, c)
        for d in range(1, NY):
            arrives_y(0, c, d).wait_recv()

    ss_mine[1] = finish_exchange(0)
    start_exchange(1)

    def both_second(i, _):
        products(offset_at(i), 1)
        send(offset_at(i), 1, 0)
        return 0

    lax.fori_loop(0, PEERS - 1, both_second, 0)
    products(0, 1)
    keep_own(1, 0)
    ss_mine[2] = finish_exchange(1)
    start_exchange(2)
    send_all(1, 1)

    def result(c, inverse):
        value = sum_y(1, c) * inverse
        out_ref[pl.ds(y * QUARTER, QUARTER), pl.ds(START[c], ROWS[c])] = value.astype(jnp.bfloat16)
        for d in range(1, NY):
            gather_y(1, c, d).start()

    inverse = None
    for c in range(CHUNKS):
        wait_arrived(1, c)
        left_products(1, c)
        for d in range(1, NY):
            scatter_y(1, c, d).start()
        own_quarter(c)
        if c + 2 < CHUNKS:
            send_all(1, c + 2)
        if c == 0:
            squares = finish_exchange(2)
            cells = PEERS * BLOCKS * B * B
            inverse = 1.0 / jnp.sqrt(jnp.sum(squares, keepdims=True) / cells + EPSILON)
        else:
            result(c - 1, inverse)
    result(CHUNKS - 1, inverse)
    for c in range(CHUNKS):
        for d in range(1, NY):
            arrives_y(1, c, d).wait_recv()

    pltpu.make_async_copy(out_of, out_of, tag_send).wait()
    for c in range(CHUNKS):
        wait_sent(1, c)
        for m in range(2):
            for d in range(1, NY):
                scatter_y(m, c, d).wait_send()
                gather_y(m, c, d).wait_send()


def body(wavefunction, energy_shift, left_env, right_env, target):
    smem, vmem = pl.BlockSpec(memory_space=pltpu.SMEM), pl.BlockSpec(memory_space=pltpu.VMEM)
    hbm = pl.BlockSpec(memory_space=pl.ANY)
    bf16, f32 = jnp.bfloat16, jnp.float32
    dma, all_chunks = pltpu.SemaphoreType.DMA, 2 * CHUNKS
    scratch = [
        pltpu.VMEM((PEERS, 8, B), jnp.int32),
        pltpu.VMEM((8, 2 * B), jnp.int32),
        pltpu.SMEM((8, 2 * B), jnp.int32),
        pltpu.VMEM((ITEMS, B, B), bf16),
        pltpu.VMEM((ITEMS, B, B), bf16),
        pltpu.VMEM((SLOTS, B, B), bf16),
        [pltpu.VMEM((SLOTS, rows, B), bf16) for rows in ROWS],
        [pltpu.VMEM((SLOTS, rows, B), bf16) for rows in 2 * ROWS],
        pltpu.VMEM((SLOTS, max(ROWS), B), f32),
        pltpu.VMEM((PEERS, 8, B), jnp.int32),
        pltpu.VMEM((8, 2 * B), jnp.int32),
        pltpu.SMEM((8, 2 * B), jnp.int32),
        [pltpu.VMEM((BLOCKS, rows, B), bf16) for rows in 2 * ROWS],
        [pltpu.VMEM((NY - 1, QUARTER, rows, B), bf16) for rows in 2 * ROWS],
        [pltpu.VMEM((QUARTER, rows, B), f32) for rows in ROWS],
        pltpu.VMEM((QUARTER, B, B), f32),
        pltpu.VMEM((BLOCKS, B, B), bf16),
        pltpu.VMEM((3, 8, B), f32),
        pltpu.VMEM((NY - 1, 8, B), f32),
        pltpu.VMEM((NX * NC - 1, 8, B), f32),
        pltpu.VMEM((NZ - 1, 8, B), f32),
        dma((2,)),
        dma,
        dma,
        dma,
        dma((2, CHUNKS)),
        dma((2, CHUNKS)),
        dma((2, CHUNKS)),
        dma((all_chunks, NY - 1)),
        dma((all_chunks, NY - 1)),
        dma((all_chunks, NY - 1)),
        dma((all_chunks, NY - 1)),
        dma((3, NZ - 1)),
        dma((3, NZ - 1)),
    ]
    transposed = pl.pallas_call(
        main_kernel,
        out_shape=jax.ShapeDtypeStruct((BLOCKS, B, B), bf16),
        in_specs=[smem, vmem, vmem, hbm, hbm],
        out_specs=vmem,
        scratch_shapes=scratch,
        compiler_params=pltpu.CompilerParams(
            collective_id=0, has_side_effects=True, vmem_limit_bytes=58 * 2**20
        ),
        name="davidson",
    )(
        energy_shift, target, wavefunction,
        right_env.reshape(ITEMS, B, B), left_env.reshape(ITEMS, B, B),
    )
    return jnp.swapaxes(transposed, 1, 2)


def solution(mesh):
    placed = (
        P("sec", None, None),
        P(),
        P("mpo", "sec", None, None),
        P("mpo", "sec", None, None),
        P("mpo", "sec"),
    )
    return jax.shard_map(
        body, mesh=mesh, in_specs=placed, out_specs=P("sec", None, None), check_vma=False
    )
```
